256 devices in a mesh: pi: 16 (over x, z_hi, core), pj: 16 (over y, z_lo).
Axes of the slice: x: 4, y: 4, z: 8 (z_hi: 2, z_lo: 4; z = z_hi * 4 + z_lo), core: 2. Of those that a mesh axis runs over, the one named last changes fastest.
Arguments:
- amplitudes: bfloat16 [32, 48, 8, 4096], P('pi', 'pj'), may hold values from -6 to 6
- coulomb: bfloat16 [48, 48, 8, 4096], P('pi', 'pj'), may hold values from -0.046875 to 0.046875
- exchange: bfloat16 [48, 48, 8, 4096], P('pi', 'pj'), may hold values from -0.046875 to 0.046875
- occ_irrep: int32 [48], replicated, may hold values from 0 to 7
Outputs:
- residual: bfloat16 [32, 48, 8, 4096], P('pi', 'pj')
The draws below stay inside these ranges and needn't reach their ends.
Inputs may be any that keep to these rules, and one draw needn't show every extreme that they name: `occ_irrep`: the virtual orbitals hold 64 of each of the 8 irreps and are stored irrep by irrep.
All inputs are finite; a program needn't handle non-finite values.
Results may differ from the reference program's by a relative error of at most 0.0058.
Values may be sent and summed in bfloat16 or wider, within the bound.
No kernel may reach another device: no remote copies, remote signals or barrier semaphores. Data moves between devices by JAX's collectives and lax.ppermute only.
A program may use at most 384 MiB of HBM per device.

```python
import jax
import jax.numpy as jnp
from jax import lax

NO = 48
NVI = 64
NI = 32


def plant(drawn, rng, least, high):
    index_at = [jax.random.randint(jax.random.fold_in(rng, axis), (), 0, length) for axis, length in enumerate(drawn.shape)]
    main_axis = drawn.shape.index(max(drawn.shape))
    neighbour = index_at[:main_axis] + [(index_at[main_axis] + 1) % drawn.shape[main_axis]] + index_at[main_axis + 1:]
    return drawn.at[tuple(index_at)].set(least).at[tuple(neighbour)].set(high)


def level_of(own_key, dims, cuts, least, top_value):
    def one(dim, shards_of):
        draws = jax.random.uniform(jax.random.fold_in(jax.random.fold_in(own_key, 6), dim), (shards_of,), jnp.float32, least / len(cuts), top_value / len(cuts))
        return jnp.repeat(jnp.exp(draws), dims[dim] // shards_of).reshape((-1,) + (1,) * (len(dims) - dim - 1))

    level = one(*cuts[0])
    for cut in cuts[1:]:
        level = level * one(*cut)
    return level


def normal_values(own_key, extent, spread, limit, pieces=(), held_as=jnp.bfloat16):
    gain = level_of(own_key, extent, pieces, -0.22, 0.18) if pieces else 1.0
    drawn = jax.random.normal(own_key, extent, jnp.float32) * spread * gain
    return jnp.minimum(jnp.maximum(drawn, -limit), limit).astype(held_as)


def setup_inputs(seed: int = 0) -> dict:
    keys = jax.random.split(jax.random.key(seed), 5)
    amplitudes = normal_values(keys[0], (NI, NO, 8, NVI * NVI), 1.0, 6.0, ((0, 16), (1, 16)))
    coulomb = normal_values(keys[1], (NO, NO, 8, NVI * NVI), (5 * NO * NVI) ** -0.5, 0.046875, ((0, 16), (1, 16)))
    exchange = normal_values(keys[2], (NO, NO, 8, NVI * NVI), (5 * NO * NVI) ** -0.5, 0.046875, ((0, 16), (1, 16)))
    occ_irrep = plant(jax.random.randint(keys[3], (NO,), 0, 8), jax.random.fold_in(keys[3], 1), 0, 7).astype(jnp.int32)
    return dict(amplitudes=amplitudes, coulomb=coulomb, exchange=exchange, occ_irrep=occ_irrep)


def reference(amplitudes, coulomb, exchange, occ_irrep):
    blocks = jnp.arange(8, dtype=jnp.int32)
    orbital = jnp.arange(NO, dtype=jnp.int32)
    first = jnp.arange(NI, dtype=jnp.int32)
    amp_blocks = amplitudes.reshape(NI, NO, 8, NVI, NVI)
    pair = jnp.bitwise_xor(occ_irrep[:, None], occ_irrep[None, :]).astype(jnp.int32)
    select_kj = jnp.bitwise_xor(blocks[None, None, :], pair[:, :, None]).astype(jnp.int32)
    select_ik = select_kj[:NI]
    swapped = amp_blocks[first[:, None, None], orbital[None, :, None], select_ik]
    doubled = (2.0 * amp_blocks.astype(jnp.float32) - jnp.swapaxes(swapped, 3, 4).astype(jnp.float32)).astype(jnp.bfloat16)
    ladder = (2.0 * coulomb.astype(jnp.float32) - exchange.astype(jnp.float32)).astype(jnp.bfloat16)
    ladder = ladder.reshape(NO, NO, 8, NVI, NVI)
    cross_ladder = ladder[orbital[:, None, None], orbital[None, :, None], select_kj]

    def one_row(packed):
        row_doubled, row_amp, row_select = packed
        direct_ladder = ladder[orbital[:, None, None], orbital[None, :, None], row_select[:, None, :]]
        direct = jnp.einsum("khac,kjhcb->jhab", row_doubled.astype(jnp.float32), direct_ladder.astype(jnp.float32))
        cross_amp = row_amp[orbital[:, None, None], select_kj]
        crossed = jnp.einsum("kjhca,kjhcb->jhab", cross_ladder.astype(jnp.float32), cross_amp.astype(jnp.float32))
        return (direct - crossed).astype(jnp.bfloat16)

    result = lax.map(one_row, (doubled, amp_blocks, select_ik))
    return result.reshape(NI, NO, 8, NVI * NVI)
```

```python
import jax
import jax.numpy as jnp
from jax import lax
from jax.experimental import pallas as pl
from jax.experimental.pallas import tpu as pltpu
from jax.sharding import PartitionSpec as P

NVI = 64
MESH_X, MESH_Y, MESH_ZH, MESH_ZL = 4, 4, 2, 4
CHUNKS = 16


def perm_pi(move):
    pairs = []
    for x in range(MESH_X):
        for zh in range(MESH_ZH):
            for c in range(2):
                x2, zh2, c2 = move(x, zh, c)
                pairs.append((x * 4 + zh * 2 + c, (x2 % 4) * 4 + zh2 * 2 + c2))
    return pairs


def perm_pj(move):
    pairs = []
    for y in range(MESH_Y):
        for zl in range(MESH_ZL):
            y2, zl2 = move(y, zl)
            pairs.append((y * 4 + zl, (y2 % 4) * 4 + zl2))
    return pairs


def shift_y(d):
    return perm_pj(lambda y, zl: (y + d, zl))


def shift_x(d):
    return perm_pi(lambda x, zh, c: (x + d, zh, c))


def swap_zl(d):
    return perm_pj(lambda y, zl: (y, zl ^ d))


SWAP_ZH = perm_pi(lambda x, zh, c: (x, zh ^ 1, c))
SWAP_CORE = perm_pi(lambda x, zh, c: (x, zh, c ^ 1))


def spread(half):
    row = lax.broadcasted_iota(jnp.int32, (512, 256), 0)
    col = lax.broadcasted_iota(jnp.int32, (512, 256), 1)
    want = ((row & 63) >> 1) * 8 + (row >> 6)
    return jnp.where((col == want) & ((row & 1) == half), 1.0, 0.0).astype(jnp.bfloat16)


def gather_back(half):
    row = lax.broadcasted_iota(jnp.int32, (256, 512), 0)
    col = lax.broadcasted_iota(jnp.int32, (256, 512), 1)
    want = ((col & 63) >> 1) * 8 + (col >> 6)
    return jnp.where((row == want) & ((col & 1) == half), 1.0, 0.0).astype(jnp.bfloat16)


def stacked(flat):
    return jnp.concatenate([flat[:, v * 128 : (v + 1) * 128] for v in range(32)], axis=0)


def amp_prep(labels, amp_ref, out_ref):
    base = lax.axis_index("pj") * 3
    picks = [spread(0), spread(1)]
    for k in range(3):
        label = labels[base + k]
        rows = [stacked(amp_ref[i, k].astype(jnp.float32)).astype(jnp.bfloat16) for i in range(2)]
        block = jnp.zeros((512, 128), jnp.float32)
        for p in range(2):
            side = jnp.concatenate([r[:, p * 64 : p * 64 + 64] for r in rows], axis=1)
            block += jnp.dot(picks[p], side, preferred_element_type=jnp.float32)
        block = block.astype(jnp.bfloat16)
        for h in range(8):
            out_ref[h ^ label, k] = block[h * 64 : h * 64 + 64]


def ladder_prep(labels, coul_ref, exch_ref, out_ref):
    base = lax.axis_index("pi") * 3
    picks = [spread(0), spread(1)]
    for k in range(3):
        label = labels[base + k]
        rows = []
        for j in range(3):
            ladder = 2.0 * coul_ref[k, j].astype(jnp.float32) - exch_ref[k, j].astype(jnp.float32)
            rows.append(stacked(ladder).astype(jnp.bfloat16))
        block = jnp.zeros((512, 192), jnp.float32)
        for p in range(2):
            side = jnp.concatenate([r[:, p * 64 : p * 64 + 64] for r in rows], axis=1)
            block += jnp.dot(picks[p], side, preferred_element_type=jnp.float32)
        for h in range(8):
            part = block[h * 64 : h * 64 + 64]
            out_ref[h ^ label, k, 0:64] = part[:, 0:128].astype(jnp.bfloat16)
            third = jnp.concatenate([part[0:32, 128:192], part[32:64, 128:192]], axis=1)
            out_ref[h ^ label, k, 64:96] = third.astype(jnp.bfloat16)


def contract(labels, *refs):
    amp_in, lad_in = refs[:CHUNKS], refs[CHUNKS : 2 * CHUNKS]
    out_ref, amp, lad, diff, cross, sems = refs[2 * CHUNKS :]
    pi, pj = lax.axis_index("pi"), lax.axis_index("pj")
    x, zh, core = pi // 4, (pi // 2) % 2, pi % 2
    y, zl = pj // 4, pj % 4
    copies = []
    for n, (s, d) in enumerate(AMP_KEYS):
        slot = ((y + 4 - s) % 4) * 4 + (zl ^ d)
        copies.append(pltpu.make_async_copy(amp_in[n], amp.at[slot], sems.at[n]))
    for n, (s, d, c) in enumerate(LAD_KEYS):
        slot = ((x + 4 - s) % 4) * 4 + (zh ^ d) * 2 + (core ^ c)
        copies.append(pltpu.make_async_copy(lad_in[n], lad.at[slot], sems.at[CHUNKS + n]))
    for copy in copies:
        copy.start()
    for copy in copies:
        copy.wait()
    label_i = [labels[pi * 2 + i] for i in range(2)]

    def one_block(hb, carry):
        first = jnp.zeros((128, 256), jnp.float32)
        second = jnp.zeros((128, 256), jnp.float32)
        for g in range(4):
            weights, left, right = [], [], []
            for k in range(12):
                m, kk = g * 4 + k // 3, k % 3
                part = lad[m, hb, kk]
                low = part[64:96]
                third = jnp.concatenate([low, pltpu.roll(low.astype(jnp.float32), 64, 1).astype(jnp.bfloat16)], axis=0)
                weights.append(jnp.concatenate([part[0:64], third], axis=1))
                right.append(amp[m, hb, kk])
            for q in range(6):
                tops = []
                for i in range(2):
                    pair = []
                    for k in (2 * q, 2 * q + 1):
                        m, kk = g * 4 + k // 3, k % 3
                        at = hb ^ label_i[i] ^ labels[m * 3 + kk]
                        pair.append(amp[m, at, kk][:, i * 64 : i * 64 + 64])
                    tops.append(jnp.concatenate(pair, axis=1))
                left.append(jnp.concatenate(tops, axis=0))
            weight = jnp.concatenate(weights, axis=0)
            first += jnp.dot(jnp.concatenate(left, axis=1), weight, preferred_element_type=jnp.float32)
            second += lax.dot_general(
                jnp.concatenate(right, axis=0), weight, (((0,), (0,)), ((), ())),
                preferred_element_type=jnp.float32,
            )
        diff[hb] = 2.0 * first - second
        cross[hb] = jnp.transpose(second)
        return carry

    lax.fori_loop(0, 8, one_block, 0)
    label_j = [labels[pj * 3 + j] for j in range(3)]
    tall = []
    for h in range(8):
        row = []
        for i in range(2):
            for j in range(3):
                direct = diff[h ^ label_i[i], i * 64 : i * 64 + 64, j * 64 : j * 64 + 64]
                crossed = cross[h ^ label_j[j], j * 64 : j * 64 + 64, i * 64 : i * 64 + 64]
                row.append(direct - crossed)
        tall.append(jnp.concatenate(row, axis=1).astype(jnp.bfloat16))
    tall = jnp.concatenate(tall, axis=0)
    sides = [jnp.dot(gather_back(p), tall, preferred_element_type=jnp.float32) for p in range(2)]
    for i in range(2):
        for j in range(3):
            at = (i * 3 + j) * 64
            both = jnp.concatenate([s[:, at : at + 64] for s in sides], axis=1)
            for v in range(32):
                out_ref[i, j, :, v * 128 : v * 128 + 128] = both[v * 8 : v * 8 + 8].astype(jnp.bfloat16)


AMP_KEYS = [(s, d) for s in range(4) for d in range(4)]
LAD_KEYS = [(s, d, c) for c in range(2) for s in range(4) for d in range(2)]


def call(kernel, shape, labels, args, spaces, scratch, flops, nbytes):
    return pl.pallas_call(
        kernel,
        out_shape=jax.ShapeDtypeStruct(shape, jnp.bfloat16),
        in_specs=[pl.BlockSpec(memory_space=pltpu.SMEM)] + [pl.BlockSpec(memory_space=s) for s in spaces],
        out_specs=pl.BlockSpec(memory_space=pltpu.VMEM),
        scratch_shapes=scratch,
        compiler_params=pltpu.CompilerParams(vmem_limit_bytes=40 * 1024 * 1024),
        cost_estimate=pl.CostEstimate(flops=flops, bytes_accessed=nbytes, transcendentals=0),
    )(labels, *args)


def prepare_amp(labels, amplitudes):
    return call(amp_prep, (8, 3, 64, 128), labels, [amplitudes], [pltpu.VMEM], [], 10**9, 10**6)


def prepare_ladder(labels, coulomb, exchange):
    return call(
        ladder_prep, (8, 3, 96, 128), labels, [coulomb, exchange], [pltpu.VMEM] * 2, [], 10**9, 2 * 10**6
    )


def finish(labels, amp, lad):
    args = [amp[key] for key in AMP_KEYS] + [lad[key] for key in LAD_KEYS]
    scratch = [
        pltpu.VMEM((CHUNKS, 8, 3, 64, 128), jnp.bfloat16),
        pltpu.VMEM((CHUNKS, 8, 3, 96, 128), jnp.bfloat16),
        pltpu.VMEM((8, 128, 256), jnp.float32),
        pltpu.VMEM((8, 256, 128), jnp.float32),
        pltpu.SemaphoreType.DMA((2 * CHUNKS,)),
    ]
    return call(
        contract, (2, 3, 8, NVI * NVI), labels, args, [pl.ANY] * (2 * CHUNKS), scratch, 5 * 10**9, 16 * 10**6
    )


def on_device(amplitudes, coulomb, exchange, occ_irrep):
    amp, lad = {}, {}
    amp[0, 0] = prepare_amp(occ_irrep, amplitudes)
    own = prepare_ladder(occ_irrep, coulomb, exchange)
    for d in (1, 2, 3):
        amp[0, d] = lax.ppermute(amp[0, 0], "pj", swap_zl(d))
    for d in range(4):
        amp[1, d] = lax.ppermute(amp[0, d], "pj", shift_y(1))
        amp[3, d] = lax.ppermute(amp[0, d], "pj", shift_y(-1))
    for d in range(4):
        if d < 2:
            amp[2, d] = lax.ppermute(amp[1, d], "pj", shift_y(1))
        else:
            amp[2, d] = lax.ppermute(amp[3, d], "pj", shift_y(-1))
    lad[0, 0, 0] = own
    lad[0, 1, 0] = lax.ppermute(own, "pi", SWAP_ZH)
    for d in range(2):
        lad[1, d, 0] = lax.ppermute(lad[0, d, 0], "pi", shift_x(1))
        lad[3, d, 0] = lax.ppermute(lad[0, d, 0], "pi", shift_x(-1))
    lad[2, 0, 0] = lax.ppermute(lad[1, 0, 0], "pi", shift_x(1))
    lad[2, 1, 0] = lax.ppermute(lad[3, 1, 0], "pi", shift_x(-1))
    for s in range(4):
        for d in range(2):
            lad[s, d, 1] = lax.ppermute(lad[s, d, 0], "pi", SWAP_CORE)
    return finish(occ_irrep, amp, lad)


def solution(mesh):
    placed = (P("pi", "pj", None, None), P("pi", "pj", None, None), P("pi", "pj", None, None), P())
    return jax.shard_map(
        on_device, mesh=mesh, in_specs=placed, out_specs=P("pi", "pj", None, None), check_vma=False
    )
```

```python
import jax
import jax.numpy as jnp
from jax import lax
from jax.experimental import pallas as pl
from jax.experimental.pallas import tpu as pltpu
from jax.sharding import PartitionSpec as P

NVI = 64
MESH_X, MESH_Y, MESH_ZH, MESH_ZL = 4, 4, 2, 4
CHUNKS = 16


def perm_pi(move):
    pairs = []
    for x in range(MESH_X):
        for zh in range(MESH_ZH):
            for c in range(2):
                x2, zh2, c2 = move(x, zh, c)
                pairs.append((x * 4 + zh * 2 + c, (x2 % 4) * 4 + zh2 * 2 + c2))
    return pairs


def perm_pj(move):
    pairs = []
    for y in range(MESH_Y):
        for zl in range(MESH_ZL):
            y2, zl2 = move(y, zl)
            pairs.append((y * 4 + zl, (y2 % 4) * 4 + zl2))
    return pairs


def shift_y(d):
    return perm_pj(lambda y, zl: (y + d, zl))


def shift_x(d):
    return perm_pi(lambda x, zh, c: (x + d, zh, c))


def swap_zl(d):
    return perm_pj(lambda y, zl: (y, zl ^ d))


SWAP_CORE = perm_pi(lambda x, zh, c: (x, zh, c ^ 1))
SWAP_ZH = perm_pi(lambda x, zh, c: (x, zh ^ 1, c))


def spread(half):
    row = lax.broadcasted_iota(jnp.int32, (512, 256), 0)
    col = lax.broadcasted_iota(jnp.int32, (512, 256), 1)
    want = ((row & 63) >> 1) * 8 + (row >> 6)
    return jnp.where((col == want) & ((row & 1) == half), 1.0, 0.0).astype(jnp.bfloat16)


def gather_back(half):
    row = lax.broadcasted_iota(jnp.int32, (256, 512), 0)
    col = lax.broadcasted_iota(jnp.int32, (256, 512), 1)
    want = ((col & 63) >> 1) * 8 + (col >> 6)
    return jnp.where((row == want) & ((col & 1) == half), 1.0, 0.0).astype(jnp.bfloat16)


def stacked(flat):
    return jnp.concatenate([flat[:, v * 128 : (v + 1) * 128] for v in range(32)], axis=0)


def prepare(labels, amp_in, coul_in, exch_in, amp_out, lad_out, amp, coul, exch, sems):
    loads = [
        pltpu.make_async_copy(source, target, sems.at[n])
        for n, (source, target) in enumerate(((amp_in, amp), (coul_in, coul), (exch_in, exch)))
    ]
    for load in loads:
        load.start()
    picks = [spread(0), spread(1)]

    def matrices(flats):
        rows = [stacked(flat).astype(jnp.bfloat16) for flat in flats]
        block = None
        for p in range(2):
            side = jnp.concatenate([r[:, p * 64 : p * 64 + 64] for r in rows], axis=1)
            part = jnp.dot(picks[p], side, preferred_element_type=jnp.float32)
            block = part if block is None else block + part
        return block

    loads[0].wait()
    base = lax.axis_index("pj") * 3
    for k in range(3):
        label = labels[base + k]
        block = matrices([amp[i, k].astype(jnp.float32) for i in range(2)]).astype(jnp.bfloat16)
        for h in range(8):
            amp_out[h ^ label, k] = block[h * 64 : h * 64 + 64]
    loads[1].wait()
    loads[2].wait()
    base = lax.axis_index("pi") * 3
    for k in range(3):
        label = labels[base + k]
        block = matrices(
            [2.0 * coul[k, j].astype(jnp.float32) - exch[k, j].astype(jnp.float32) for j in range(3)]
        )
        for h in range(8):
            part = block[h * 64 : h * 64 + 64]
            lad_out[h ^ label, k, 0:64] = part[:, 0:128].astype(jnp.bfloat16)
            third = jnp.concatenate([part[0:32, 128:192], part[32:64, 128:192]], axis=1)
            lad_out[h ^ label, k, 64:96] = third.astype(jnp.bfloat16)


def halves(x, y):
    late0, late1 = (x + 2) % 4, (y + 2) % 4
    late1 = jnp.where(late1 == late0, (late0 + 1) % 4, late1)
    early0 = jnp.where((late0 + 1) % 4 == late1, (late0 + 2) % 4, (late0 + 1) % 4)
    return (early0, 6 - late0 - late1 - early0), (late0, late1)


def products(labels, amp_in, lad_in, amp_parts, lad_parts, amp, lad, sems, late, one_block):
    pi, pj = lax.axis_index("pi"), lax.axis_index("pj")
    x, zh, core = pi // 4, (pi // 2) % 2, pi % 2
    y, zl = pj // 4, pj % 4
    columns = halves(x, y)[late]
    copies = []

    def bring(source, target, mx, group):
        copy = pltpu.make_async_copy(source, target, sems.at[len(copies)])
        copies.append((copy, (mx == columns[0]) | (mx == columns[1]), group))

    for name, first, (s, d), h, count in amp_parts:
        mx = (y + 4 - s) % 4
        slot = jnp.where(mx == columns[0], 0, 4) + (zl ^ d)
        bring(amp_in[name].at[pl.ds(first, count)], amp.at[slot, pl.ds(h, count)], mx, 0)
    for half in range(2):
        for name, first, (s, d, c) in lad_parts:
            mx = (x + 4 - s) % 4
            slot = jnp.where(mx == columns[0], 0, 4) + (zh ^ d) * 2 + (core ^ c)
            bring(
                lad_in[name].at[pl.ds(first + half * 4, 4)], lad.at[slot, pl.ds(half * 4, 4)], mx, half
            )
    for copy, wanted, _ in copies:
        pl.when(wanted)(copy.start)

    label_i = [labels[pi * 2 + i] for i in range(2)]

    def block(hb, carry):
        first = jnp.zeros((128, 256), jnp.float32)
        second = jnp.zeros((128, 256), jnp.float32)
        for g in range(2):
            weights, left, right = [], [], []
            for k in range(12):
                m, kk = g * 4 + k // 3, k % 3
                part = lad[m, hb, kk]
                low = part[64:96]
                turned = pltpu.roll(low.astype(jnp.float32), 64, 1).astype(jnp.bfloat16)
                weights.append(jnp.concatenate([part[0:64], jnp.concatenate([low, turned], axis=0)], axis=1))
                right.append(amp[m, hb, kk])
            for q in range(6):
                tops = []
                for i in range(2):
                    pair = []
                    for k in (2 * q, 2 * q + 1):
                        m, kk = g * 4 + k // 3, k % 3
                        label = labels[(columns[g] * 4 + k // 3) * 3 + kk]
                        pair.append(amp[m, hb ^ label_i[i] ^ label, kk][:, i * 64 : i * 64 + 64])
                    tops.append(jnp.concatenate(pair, axis=1))
                left.append(jnp.concatenate(tops, axis=0))
            weight = jnp.concatenate(weights, axis=0)
            first += jnp.dot(jnp.concatenate(left, axis=1), weight, preferred_element_type=jnp.float32)
            second += lax.dot_general(
                jnp.concatenate(right, axis=0), weight, (((0,), (0,)), ((), ())),
                preferred_element_type=jnp.float32,
            )
        one_block(hb, first, second)
        return carry

    for half in range(2):
        for copy, wanted, group in copies:
            if group == half:
                pl.when(wanted)(copy.wait)
        lax.fori_loop(half * 4, half * 4 + 4, block, 0)


def early_products(labels, *refs):
    amp_in = dict(zip(AMP_EARLY, refs))
    lad_in = dict(zip(LAD_EARLY, refs[len(AMP_EARLY) :]))
    first_out, second_out, amp, lad, sems = refs[len(AMP_EARLY) + len(LAD_EARLY) :]

    def keep(hb, first, second):
        first_out[hb] = first
        second_out[hb] = second

    amp_parts = [part for part in AMP_PARTS if part[2][0] != 2]
    lad_parts = [part for part in LAD_PARTS if part[2][0] != 2]
    products(labels, amp_in, lad_in, amp_parts, lad_parts, amp, lad, sems, 0, keep)


def late_products(labels, first_in, second_in, *refs):
    amp_in = dict(zip(AMP_NAMES, refs))
    lad_in = dict(zip(LAD_NAMES, refs[len(AMP_NAMES) :]))
    out_ref, amp, lad, diff, cross, sems = refs[len(AMP_NAMES) + len(LAD_NAMES) :]
    pi, pj = lax.axis_index("pi"), lax.axis_index("pj")

    def keep(hb, first, second):
        second = second + second_in[hb]
        diff[hb] = 2.0 * (first + first_in[hb]) - second
        cross[hb] = jnp.transpose(second)

    products(labels, amp_in, lad_in, AMP_PARTS, LAD_PARTS, amp, lad, sems, 1, keep)
    label_i = [labels[pi * 2 + i] for i in range(2)]
    label_j = [labels[pj * 3 + j] for j in range(3)]
    tall = []
    for h in range(8):
        row = []
        for i in range(2):
            for j in range(3):
                direct = diff[h ^ label_i[i], i * 64 : i * 64 + 64, j * 64 : j * 64 + 64]
                crossed = cross[h ^ label_j[j], j * 64 : j * 64 + 64, i * 64 : i * 64 + 64]
                row.append(direct - crossed)
        tall.append(jnp.concatenate(row, axis=1).astype(jnp.bfloat16))
    tall = jnp.concatenate(tall, axis=0)
    sides = [jnp.dot(gather_back(p), tall, preferred_element_type=jnp.float32) for p in range(2)]
    for i in range(2):
        for j in range(3):
            at = (i * 3 + j) * 64
            both = jnp.concatenate([s[:, at : at + 64] for s in sides], axis=1)
            for v in range(32):
                out_ref[i, j, :, v * 128 : v * 128 + 128] = both[v * 8 : v * 8 + 8].astype(jnp.bfloat16)


AMP_PARTS = [
    ("a", 0, (0, 0), 0, 8), ("z1", 0, (0, 1), 0, 8), ("z2", 0, (0, 2), 0, 8), ("z3", 0, (0, 3), 0, 8),
    ("yo+", 0, (1, 0), 0, 8), ("yo-", 0, (3, 0), 0, 8), ("fo", 0, (2, 0), 0, 8),
    ("yq+", 0, (1, 1), 0, 8), ("yq+", 8, (1, 2), 0, 8), ("yq-", 0, (3, 1), 0, 8), ("yq-", 8, (3, 2), 0, 8),
    ("f1", 0, (2, 1), 0, 8), ("f2", 0, (2, 2), 0, 8),
    ("y3+", 0, (1, 3), 0, 8), ("y3-", 0, (3, 3), 0, 8), ("f3a", 0, (2, 3), 0, 4), ("f3b", 0, (2, 3), 4, 4),
]
LAD_PARTS = [
    ("l", 0, (0, 0, 0)), ("xo+", 0, (1, 0, 0)), ("xo-", 0, (3, 0, 0)), ("fxo", 0, (2, 0, 0)),
    ("zh", 0, (0, 1, 0)), ("xz+", 0, (1, 1, 0)), ("xz-", 0, (3, 1, 0)), ("fxz", 0, (2, 1, 0)),
    ("c1", 0, (0, 0, 1)), ("c1", 8, (1, 0, 1)), ("c1", 16, (3, 0, 1)),
    ("c1", 24, (0, 1, 1)), ("c1", 32, (1, 1, 1)), ("c1", 40, (3, 1, 1)),
    ("c2", 0, (2, 0, 1)), ("c2", 8, (2, 1, 1)),
]
AMP_NAMES = list(dict.fromkeys(part[0] for part in AMP_PARTS))
LAD_NAMES = list(dict.fromkeys(part[0] for part in LAD_PARTS))
AMP_EARLY = list(dict.fromkeys(part[0] for part in AMP_PARTS if part[2][0] != 2))
LAD_EARLY = list(dict.fromkeys(part[0] for part in LAD_PARTS if part[2][0] != 2))
COPIES = len(AMP_PARTS) + 2 * len(LAD_PARTS)
X_UP, X_DOWN = ("pi", shift_x(1)), ("pi", shift_x(-1))
Y_UP, Y_DOWN, Y_FAR = ("pj", shift_y(1)), ("pj", shift_y(-1)), ("pj", shift_y(2))
Z_ONE, Z_TWO = ("pj", swap_zl(1)), ("pj", swap_zl(2))
Z_HALF, OTHER_CORE = ("pi", SWAP_ZH), ("pi", SWAP_CORE)
PLAN = [
    ("z1", "a", Z_ONE, 0, 1),
    ("z2", "a", Z_TWO, 0, 1),
    ("yo+", "a", Y_UP, 0, 1),
    ("yo-", "a", Y_DOWN, 0, 1),
    ("xo+", "l", X_UP, 0, 1),
    ("zh", "l", Z_HALF, 1, 2),
    ("yq+", ("z1", "z2"), Y_UP, 1, 2),
    ("yq-", ("z1", "z2"), Y_DOWN, 1, 2),
    ("fo", "yo+", Y_UP, 1, 2),
    ("xo-", "l", X_DOWN, 1, 2),
    ("z3", "z2", Z_ONE, 2, 3),
    ("f1", ("yq+", 0, 8), Y_UP, 2, 3),
    ("f2", ("yq-", 8, 16), Y_DOWN, 2, 3),
    ("xz+", "zh", X_UP, 2, 3),
    ("xz-", "zh", X_DOWN, 2, 3),
    ("y3+", "z3", Y_UP, 3, 4),
    ("y3-", "z3", Y_DOWN, 3, 4),
    ("fxo", "xo+", X_UP, 3, 4),
    ("fxz", "xz-", X_DOWN, 3, 4),
    ("c1", ("l", "xo+", "xo-", "zh", "xz+", "xz-"), OTHER_CORE, 3, 4),
    ("f3a", ("y3+", 0, 4), Y_UP, 4, 5),
    ("f3b", ("y3-", 4, 8), Y_DOWN, 4, 5),
    ("c2", ("fxo", "fxz"), OTHER_CORE, 4, 5),
]
JOINS = {}


def call(kernel, outs, labels, args, spaces, scratch, flops, nbytes, vmem):
    return pl.pallas_call(
        kernel,
        out_shape=outs,
        in_specs=[pl.BlockSpec(memory_space=pltpu.SMEM)] + [pl.BlockSpec(memory_space=s) for s in spaces],
        out_specs=[pl.BlockSpec(memory_space=pltpu.VMEM)] * len(outs),
        scratch_shapes=scratch,
        compiler_params=pltpu.CompilerParams(vmem_limit_bytes=vmem * 1024 * 1024),
        cost_estimate=pl.CostEstimate(flops=flops, bytes_accessed=nbytes, transcendentals=0),
    )(labels, *args)


def lay_out(labels, *args):
    scratch = [pltpu.VMEM(arg.shape, arg.dtype) for arg in args] + [pltpu.SemaphoreType.DMA((3,))]
    outs = [jax.ShapeDtypeStruct((8, 3, rows, 128), jnp.bfloat16) for rows in (64, 96)]
    return call(prepare, outs, labels, args, [pl.ANY] * 3, scratch, 2 * 10**9, 3 * 10**6, 60)


def slots():
    return [pltpu.VMEM((8, 8, 3, 64, 128), jnp.bfloat16), pltpu.VMEM((8, 8, 3, 96, 128), jnp.bfloat16)]


def begin(labels, got):
    args = [fetch(got, name) for name in AMP_EARLY + LAD_EARLY]
    outs = [jax.ShapeDtypeStruct((8, 128, 256), jnp.float32)] * 2
    scratch = slots() + [pltpu.SemaphoreType.DMA((COPIES,))]
    return call(early_products, outs, labels, args, [pl.ANY] * len(args), scratch, 5 * 10**9, 8 * 10**6, 18)


def finish(labels, got, sums):
    args = [fetch(got, name) for name in AMP_NAMES + LAD_NAMES]
    outs = [jax.ShapeDtypeStruct((2, 3, 8, NVI * NVI), jnp.bfloat16)]
    scratch = slots() + [
        pltpu.VMEM((8, 128, 256), jnp.float32),
        pltpu.VMEM((8, 256, 128), jnp.float32),
        pltpu.SemaphoreType.DMA((COPIES,)),
    ]
    spaces = [pltpu.VMEM] * 2 + [pl.ANY] * len(args)
    return call(late_products, outs, labels, [*sums, *args], spaces, scratch, 5 * 10**9, 8 * 10**6, 22)[0]


def fetch(got, source):
    if isinstance(source, str) and source in JOINS:
        source = JOINS[source]
    if isinstance(source, str):
        return got[source]
    if isinstance(source[1], int):
        return got[source[0]][source[1] : source[2]]
    return jnp.concatenate([fetch(got, part) for part in source], axis=0)


def on_device(amplitudes, coulomb, exchange, occ_irrep):
    got = dict(zip("al", lay_out(occ_irrep, amplitudes, coulomb, exchange)))
    ends = {name: end for name, _, _, _, end in PLAN}
    starts = {name: start for name, _, _, start, _ in PLAN}
    for name, source, (axis, pairs), start, _ in sorted(PLAN, key=lambda step: step[3]):
        before = [n for n in ends if ends[n] <= start]
        last = [n for n in before if not any(ends[n] <= starts[m] for m in before)]
        value = fetch(got, source)
        if last:
            value = lax.optimization_barrier((value, *[got[n] for n in last]))[0]
        got[name] = lax.ppermute(value, axis, pairs)
    return finish(occ_irrep, got, begin(occ_irrep, got))


def solution(mesh):
    placed = (P("pi", "pj", None, None), P("pi", "pj", None, None), P("pi", "pj", None, None), P())
    return jax.shard_map(
        on_device, mesh=mesh, in_specs=placed, out_specs=P("pi", "pj", None, None), check_vma=False
    )
```

```python
import jax
import jax.numpy as jnp
from jax import lax
from jax.experimental import pallas as pl
from jax.experimental.pallas import tpu as pltpu
from jax.sharding import PartitionSpec as P

NVI = 64
UNROLL = 2
MESH_X, MESH_Y, MESH_ZH, MESH_ZL = 4, 4, 2, 4
CHUNKS = 16


def perm_pi(move):
    pairs = []
    for x in range(MESH_X):
        for zh in range(MESH_ZH):
            for c in range(2):
                x2, zh2, c2 = move(x, zh, c)
                pairs.append((x * 4 + zh * 2 + c, (x2 % 4) * 4 + zh2 * 2 + c2))
    return pairs


def perm_pj(move):
    pairs = []
    for y in range(MESH_Y):
        for zl in range(MESH_ZL):
            y2, zl2 = move(y, zl)
            pairs.append((y * 4 + zl, (y2 % 4) * 4 + zl2))
    return pairs


def shift_y(d):
    return perm_pj(lambda y, zl: (y + d, zl))


def shift_x(d):
    return perm_pi(lambda x, zh, c: (x + d, zh, c))


def swap_zl(d):
    return perm_pj(lambda y, zl: (y, zl ^ d))


SWAP_CORE = perm_pi(lambda x, zh, c: (x, zh, c ^ 1))
SWAP_ZH = perm_pi(lambda x, zh, c: (x, zh ^ 1, c))


def spread(half):
    row = lax.broadcasted_iota(jnp.int32, (512, 1), 0)
    want = jnp.where((row & 1) == half, ((row & 63) >> 1) * 8 + (row >> 6), -1)
    col = lax.broadcasted_iota(jnp.int32, (512, 256), 1)
    return jnp.where(col == want, 1.0, 0.0).astype(jnp.bfloat16)


def gather_back(half):
    col = lax.broadcasted_iota(jnp.int32, (1, 512), 1)
    want = jnp.where((col & 1) == half, ((col & 63) >> 1) * 8 + (col >> 6), -1)
    row = lax.broadcasted_iota(jnp.int32, (256, 512), 0)
    return jnp.where(row == want, 1.0, 0.0).astype(jnp.bfloat16)


def stacked(flat):
    return jnp.concatenate([flat[:, v * 128 : (v + 1) * 128] for v in range(32)], axis=0)


def prepare(labels, amp_in, coul_in, exch_in, amp_out, lad_out, amp, coul, exch, sems):
    loads = [
        pltpu.make_async_copy(source, target, sems.at[n])
        for n, (source, target) in enumerate(((amp_in, amp), (coul_in, coul), (exch_in, exch)))
    ]
    for load in loads:
        load.start()
    picks = [spread(0), spread(1)]

    def matrices(flats):
        rows = [stacked(flat).astype(jnp.bfloat16) for flat in flats]
        block = None
        for p in range(2):
            side = jnp.concatenate([r[:, p * 64 : p * 64 + 64] for r in rows], axis=1)
            part = jnp.dot(picks[p], side, preferred_element_type=jnp.float32)
            block = part if block is None else block + part
        return block

    loads[0].wait()
    base = lax.axis_index("pj") * 3
    for k in range(3):
        label = labels[base + k]
        block = matrices([amp[i, k].astype(jnp.float32) for i in range(2)]).astype(jnp.bfloat16)
        for h in range(8):
            amp_out[h ^ label, k] = block[h * 64 : h * 64 + 64]
    loads[1].wait()
    loads[2].wait()
    base = lax.axis_index("pi") * 3
    for k in range(3):
        label = labels[base + k]
        block = matrices(
            [2.0 * coul[k, j].astype(jnp.float32) - exch[k, j].astype(jnp.float32) for j in range(3)]
        )
        for h in range(8):
            part = block[h * 64 : h * 64 + 64]
            lad_out[h ^ label, k, 0:64] = part[:, 0:128].astype(jnp.bfloat16)
            third = jnp.concatenate([part[0:32, 128:192], part[32:64, 128:192]], axis=1)
            lad_out[h ^ label, k, 64:96] = third.astype(jnp.bfloat16)


def halves(x, y):
    late0, late1 = (x + 2) % 4, (y + 2) % 4
    late1 = jnp.where(late1 == late0, (late0 + 1) % 4, late1)
    early0 = jnp.where((late0 + 1) % 4 == late1, (late0 + 2) % 4, (late0 + 1) % 4)
    return (early0, 6 - late0 - late1 - early0), (late0, late1)


def products(labels, amp_in, lad_in, amp_parts, lad_parts, amp, lad, sems, late, one_block):
    pi, pj = lax.axis_index("pi"), lax.axis_index("pj")
    x, zh, core = pi // 4, (pi // 2) % 2, pi % 2
    y, zl = pj // 4, pj % 4
    columns = halves(x, y)[late]
    copies = []

    def bring(source, target, mx, group):
        copy = pltpu.make_async_copy(source, target, sems.at[len(copies)])
        copies.append((copy, (mx == columns[0]) | (mx == columns[1]), group))

    for name, first, (s, d), h, count in amp_parts:
        mx = (y + 4 - s) % 4
        slot = jnp.where(mx == columns[0], 0, 4) + (zl ^ d)
        bring(amp_in[name].at[pl.ds(first, count)], amp.at[slot, pl.ds(h, count)], mx, 0)
    for half in range(2):
        for name, first, (s, d, c), h, count in lad_parts:
            if count == 4 and h != half * 4:
                continue
            mx = (x + 4 - s) % 4
            first = first + half * 4 - h
            slot = jnp.where(mx == columns[0], 0, 4) + (zh ^ d) * 2 + (core ^ c)
            bring(lad_in[name].at[pl.ds(first, 4)], lad.at[slot, pl.ds(half * 4, 4)], mx, half)
    for copy, wanted, _ in copies:
        pl.when(wanted)(copy.start)

    label_i = [labels[pi * 2 + i] for i in range(2)]

    def block(hb, carry):
        first = jnp.zeros((128, 256), jnp.float32)
        second = jnp.zeros((128, 256), jnp.float32)
        for g in range(2):
            weights, left, right = [], [], []
            for k in range(12):
                m, kk = g * 4 + k // 3, k % 3
                part = lad[m, hb, kk]
                low = part[64:96]
                turned = pltpu.roll(low.astype(jnp.float32), 64, 1).astype(jnp.bfloat16)
                weights.append(jnp.concatenate([part[0:64], jnp.concatenate([low, turned], axis=0)], axis=1))
                right.append(amp[m, hb, kk])
            for q in range(6):
                tops = []
                for i in range(2):
                    pair = []
                    for k in (2 * q, 2 * q + 1):
                        m, kk = g * 4 + k // 3, k % 3
                        label = labels[(columns[g] * 4 + k // 3) * 3 + kk]
                        pair.append(amp[m, hb ^ label_i[i] ^ label, kk][:, i * 64 : i * 64 + 64])
                    tops.append(jnp.concatenate(pair, axis=1))
                left.append(jnp.concatenate(tops, axis=0))
            weight = jnp.concatenate(weights, axis=0)
            first += jnp.dot(jnp.concatenate(left, axis=1), weight, preferred_element_type=jnp.float32)
            second += lax.dot_general(
                jnp.concatenate(right, axis=0), weight, (((0,), (0,)), ((), ())),
                preferred_element_type=jnp.float32,
            )
        one_block(hb, first, second)
        return carry

    for half in range(2):
        for copy, wanted, group in copies:
            if group == half:
                pl.when(wanted)(copy.wait)
        lax.fori_loop(half * 4, half * 4 + 4, block, 0, unroll=UNROLL)


def early_products(labels, *refs):
    amp_in = dict(zip(AMP_EARLY, refs))
    lad_in = dict(zip(LAD_EARLY, refs[len(AMP_EARLY) :]))
    first_out, second_out, amp, lad, sems = refs[len(AMP_EARLY) + len(LAD_EARLY) :]

    def keep(hb, first, second):
        first_out[hb] = first
        second_out[hb] = second

    amp_parts = [part for part in AMP_PARTS if part[2][0] != 2]
    lad_parts = [part for part in LAD_PARTS if part[2][0] != 2]
    products(labels, amp_in, lad_in, amp_parts, lad_parts, amp, lad, sems, 0, keep)


def late_products(labels, first_in, second_in, *refs):
    amp_in = dict(zip(AMP_NAMES, refs))
    lad_in = dict(zip(LAD_NAMES, refs[len(AMP_NAMES) :]))
    out_ref, amp, lad, diff, cross, sems = refs[len(AMP_NAMES) + len(LAD_NAMES) :]
    pi, pj = lax.axis_index("pi"), lax.axis_index("pj")

    def keep(hb, first, second):
        second = second + second_in[hb]
        diff[hb] = 2.0 * (first + first_in[hb]) - second
        cross[hb] = jnp.transpose(second)

    products(labels, amp_in, lad_in, AMP_PARTS, LAD_PARTS, amp, lad, sems, 1, keep)
    label_i = [labels[pi * 2 + i] for i in range(2)]
    label_j = [labels[pj * 3 + j] for j in range(3)]
    tall = []
    for h in range(8):
        row = []
        for i in range(2):
            for j in range(3):
                direct = diff[h ^ label_i[i], i * 64 : i * 64 + 64, j * 64 : j * 64 + 64]
                crossed = cross[h ^ label_j[j], j * 64 : j * 64 + 64, i * 64 : i * 64 + 64]
                row.append(direct - crossed)
        tall.append(jnp.concatenate(row, axis=1).astype(jnp.bfloat16))
    tall = jnp.concatenate(tall, axis=0)
    sides = [jnp.dot(gather_back(p), tall, preferred_element_type=jnp.float32) for p in range(2)]
    for i in range(2):
        for j in range(3):
            at = (i * 3 + j) * 64
            both = jnp.concatenate([s[:, at : at + 64] for s in sides], axis=1)
            for v in range(32):
                out_ref[i, j, :, v * 128 : v * 128 + 128] = both[v * 8 : v * 8 + 8].astype(jnp.bfloat16)


AMP_PARTS = [
    ("a", 0, (0, 0), 0, 8), ("z1", 0, (0, 1), 0, 8), ("z2", 0, (0, 2), 0, 8), ("z3", 0, (0, 3), 0, 8),
    ("yo+", 0, (1, 0), 0, 8), ("yo-", 0, (3, 0), 0, 8), ("fo", 0, (2, 0), 0, 8),
    ("yq+", 0, (1, 1), 0, 8), ("yq+", 8, (1, 2), 0, 8), ("yq-", 0, (3, 1), 0, 8), ("yq-", 8, (3, 2), 0, 8),
    ("f1", 0, (2, 1), 0, 8), ("f2", 0, (2, 2), 0, 8),
    ("y3+", 0, (1, 3), 0, 8), ("y3-", 0, (3, 3), 0, 8), ("f3", 0, (2, 3), 0, 8),
]
LAD_PARTS = [
    ("l", 0, (0, 0, 0), 0, 8), ("xo+", 0, (1, 0, 0), 0, 8), ("xo-", 0, (3, 0, 0), 0, 8), ("fxo", 0, (2, 0, 0), 0, 8),
    ("zh", 0, (0, 1, 0), 0, 8), ("xz+", 0, (1, 1, 0), 0, 8), ("xz-", 0, (3, 1, 0), 0, 8),
    ("fxz+", 0, (2, 1, 0), 0, 4), ("fxz-", 0, (2, 1, 0), 4, 4),
    ("c1", 0, (0, 0, 1), 0, 8), ("c1", 8, (1, 0, 1), 0, 8), ("c1", 16, (3, 0, 1), 0, 8),
    ("c1", 24, (0, 1, 1), 0, 8), ("c1", 32, (1, 1, 1), 0, 8), ("c1", 40, (3, 1, 1), 0, 8),
    ("c2", 0, (2, 0, 1), 0, 8), ("c2", 8, (2, 1, 1), 0, 8),
]
AMP_NAMES = list(dict.fromkeys(part[0] for part in AMP_PARTS))
LAD_NAMES = list(dict.fromkeys(part[0] for part in LAD_PARTS))
AMP_EARLY = list(dict.fromkeys(part[0] for part in AMP_PARTS if part[2][0] != 2))
LAD_EARLY = list(dict.fromkeys(part[0] for part in LAD_PARTS if part[2][0] != 2))
COPIES = len(AMP_PARTS) + 2 * len(LAD_PARTS)
X_UP, X_DOWN = ("pi", shift_x(1)), ("pi", shift_x(-1))
Y_UP, Y_DOWN, Y_FAR = ("pj", shift_y(1)), ("pj", shift_y(-1)), ("pj", shift_y(2))
Z_ONE, Z_TWO = ("pj", swap_zl(1)), ("pj", swap_zl(2))
Z_HALF, OTHER_CORE = ("pi", SWAP_ZH), ("pi", SWAP_CORE)
PLAN = [
    ("z1", "a", Z_ONE, 0, 1),
    ("z2", "a", Z_TWO, 0, 1),
    ("yo+", "a", Y_UP, 0, 1),
    ("yo-", "a", Y_DOWN, 0, 1),
    ("xo+", "l", X_UP, 0, 1),
    ("zh", "l", Z_HALF, 1, 2),
    ("yq+", ("z1", "z2"), Y_UP, 1, 2),
    ("yq-", ("z1", "z2"), Y_DOWN, 1, 2),
    ("xo-", "l", X_DOWN, 1, 2),
    ("fxo", "xo+", X_UP, 1, 2),
    ("z3", "z2", Z_ONE, 2, 3),
    ("f1", ("yq+", 0, 8), Y_UP, 2, 3),
    ("f2", ("yq-", 8, 16), Y_DOWN, 2, 3),
    ("xz+", "zh", X_UP, 2, 3),
    ("xz-", "zh", X_DOWN, 2, 3),
    ("y3+", "z3", Y_UP, 3, 4),
    ("y3-", "z3", Y_DOWN, 3, 4),
    ("fxz+", ("xz+", 0, 4), X_UP, 3, 4),
    ("fxz-", ("xz-", 4, 8), X_DOWN, 3, 4),
    ("c1", ("l", "xo+", "xo-", "zh", "xz+", "xz-"), OTHER_CORE, 3, 4),
    ("f3", "y3+", Y_UP, 4, 5),
    ("fo", "yo-", Y_DOWN, 4, 5),
    ("c2", ("fxo", "fxz+", "fxz-"), OTHER_CORE, 4, 5),
]
JOINS = {}


def call(kernel, outs, labels, args, spaces, scratch, flops, nbytes, vmem):
    return pl.pallas_call(
        kernel,
        out_shape=outs,
        in_specs=[pl.BlockSpec(memory_space=pltpu.SMEM)] + [pl.BlockSpec(memory_space=s) for s in spaces],
        out_specs=[pl.BlockSpec(memory_space=pltpu.VMEM)] * len(outs),
        scratch_shapes=scratch,
        compiler_params=pltpu.CompilerParams(vmem_limit_bytes=vmem * 1024 * 1024),
        cost_estimate=pl.CostEstimate(flops=flops, bytes_accessed=nbytes, transcendentals=0),
    )(labels, *args)


def lay_out(labels, *args):
    scratch = [pltpu.VMEM(arg.shape, arg.dtype) for arg in args] + [pltpu.SemaphoreType.DMA((3,))]
    outs = [jax.ShapeDtypeStruct((8, 3, rows, 128), jnp.bfloat16) for rows in (64, 96)]
    return call(prepare, outs, labels, args, [pl.ANY] * 3, scratch, 2 * 10**9, 3 * 10**6, 60)


def slots():
    return [pltpu.VMEM((8, 8, 3, 64, 128), jnp.bfloat16), pltpu.VMEM((8, 8, 3, 96, 128), jnp.bfloat16)]


def begin(labels, got):
    args = [fetch(got, name) for name in AMP_EARLY + LAD_EARLY]
    outs = [jax.ShapeDtypeStruct((8, 128, 256), jnp.float32)] * 2
    scratch = slots() + [pltpu.SemaphoreType.DMA((COPIES,))]
    return call(early_products, outs, labels, args, [pl.ANY] * len(args), scratch, 5 * 10**9, 8 * 10**6, 18)


def finish(labels, got, sums):
    args = [fetch(got, name) for name in AMP_NAMES + LAD_NAMES]
    outs = [jax.ShapeDtypeStruct((2, 3, 8, NVI * NVI), jnp.bfloat16)]
    scratch = slots() + [
        pltpu.VMEM((8, 128, 256), jnp.float32),
        pltpu.VMEM((8, 256, 128), jnp.float32),
        pltpu.SemaphoreType.DMA((COPIES,)),
    ]
    spaces = [pltpu.VMEM] * 2 + [pl.ANY] * len(args)
    return call(late_products, outs, labels, [*sums, *args], spaces, scratch, 5 * 10**9, 8 * 10**6, 22)[0]


def fetch(got, source):
    if isinstance(source, str) and source in JOINS:
        source = JOINS[source]
    if isinstance(source, str):
        return got[source]
    if isinstance(source[1], int):
        return got[source[0]][source[1] : source[2]]
    return jnp.concatenate([fetch(got, part) for part in source], axis=0)


def on_device(amplitudes, coulomb, exchange, occ_irrep):
    got = dict(zip("al", lay_out(occ_irrep, amplitudes, coulomb, exchange)))
    ends = {name: end for name, _, _, _, end in PLAN}
    starts = {name: start for name, _, _, start, _ in PLAN}
    for name, source, (axis, pairs), start, _ in sorted(PLAN, key=lambda step: step[3]):
        before = [n for n in ends if ends[n] <= start]
        last = [n for n in before if not any(ends[n] <= starts[m] for m in before)]
        value = fetch(got, source)
        if last:
            value = lax.optimization_barrier((value, *[got[n] for n in last]))[0]
        got[name] = lax.ppermute(value, axis, pairs)
    return finish(occ_irrep, got, begin(occ_irrep, got))


def solution(mesh):
    placed = (P("pi", "pj", None, None), P("pi", "pj", None, None), P("pi", "pj", None, None), P())
    return jax.shard_map(
        on_device, mesh=mesh, in_specs=placed, out_specs=P("pi", "pj", None, None), check_vma=False
    )
```

```python
import jax
import jax.numpy as jnp
from jax import lax
from jax.experimental import pallas as pl
from jax.experimental.pallas import tpu as pltpu
from jax.sharding import PartitionSpec as P

NVI = 64
MESH_X, MESH_Y, MESH_ZH, MESH_ZL = 4, 4, 2, 4
CHUNKS = 16


def perm_pi(move):
    pairs = []
    for x in range(MESH_X):
        for zh in range(MESH_ZH):
            for c in range(2):
                x2, zh2, c2 = move(x, zh, c)
                pairs.append((x * 4 + zh * 2 + c, (x2 % 4) * 4 + zh2 * 2 + c2))
    return pairs


def perm_pj(move):
    pairs = []
    for y in range(MESH_Y):
        for zl in range(MESH_ZL):
            y2, zl2 = move(y, zl)
            pairs.append((y * 4 + zl, (y2 % 4) * 4 + zl2))
    return pairs


def shift_y(d):
    return perm_pj(lambda y, zl: (y + d, zl))


def shift_x(d):
    return perm_pi(lambda x, zh, c: (x + d, zh, c))


def swap_zl(d):
    return perm_pj(lambda y, zl: (y, zl ^ d))


SWAP_CORE = perm_pi(lambda x, zh, c: (x, zh, c ^ 1))
SWAP_ZH = perm_pi(lambda x, zh, c: (x, zh ^ 1, c))


def spread(half):
    row = lax.broadcasted_iota(jnp.int32, (512, 1), 0)
    want = jnp.where((row & 1) == half, ((row & 63) >> 1) * 8 + (row >> 6), -1)
    col = lax.broadcasted_iota(jnp.int32, (512, 256), 1)
    return jnp.where(col == want, 1.0, 0.0).astype(jnp.bfloat16)


def gather_back(half):
    col = lax.broadcasted_iota(jnp.int32, (1, 512), 1)
    want = jnp.where((col & 1) == half, ((col & 63) >> 1) * 8 + (col >> 6), -1)
    row = lax.broadcasted_iota(jnp.int32, (256, 512), 0)
    return jnp.where(row == want, 1.0, 0.0).astype(jnp.bfloat16)


def stacked(flat):
    return jnp.concatenate([flat[:, v * 128 : (v + 1) * 128] for v in range(32)], axis=0)


def prepare(labels, amp_in, coul_in, exch_in, amp_out, lad_out, amp, coul, exch, sems):
    loads = [
        pltpu.make_async_copy(source, target, sems.at[n])
        for n, (source, target) in enumerate(((amp_in, amp), (coul_in, coul), (exch_in, exch)))
    ]
    for load in loads:
        load.start()
    picks = [spread(0), spread(1)]

    def matrices(flats):
        rows = [stacked(flat).astype(jnp.bfloat16) for flat in flats]
        block = None
        for p in range(2):
            side = jnp.concatenate([r[:, p * 64 : p * 64 + 64] for r in rows], axis=1)
            part = jnp.dot(picks[p], side, preferred_element_type=jnp.float32)
            block = part if block is None else block + part
        return block

    loads[0].wait()
    base = lax.axis_index("pj") * 3
    for k in range(3):
        label = labels[base + k]
        block = matrices([amp[i, k].astype(jnp.float32) for i in range(2)]).astype(jnp.bfloat16)
        for h in range(8):
            amp_out[h ^ label, k] = block[h * 64 : h * 64 + 64]
    loads[1].wait()
    loads[2].wait()
    base = lax.axis_index("pi") * 3
    for k in range(3):
        label = labels[base + k]
        block = matrices(
            [2.0 * coul[k, j].astype(jnp.float32) - exch[k, j].astype(jnp.float32) for j in range(3)]
        )
        for h in range(8):
            part = block[h * 64 : h * 64 + 64]
            lad_out[h ^ label, k, 0:64] = part[:, 0:128].astype(jnp.bfloat16)
            third = jnp.concatenate([part[0:32, 128:192], part[32:64, 128:192]], axis=1)
            lad_out[h ^ label, k, 64:96] = third.astype(jnp.bfloat16)


def where_am_i():
    pi, pj = lax.axis_index("pi"), lax.axis_index("pj")
    return pi // 4, (pi // 2) % 2, pi % 2, pj // 4, pj % 4


def columns(x, y):
    far_x, far_y = (x + 2) % 4, (y + 2) % 4
    third = jnp.where(far_y == far_x, (far_x + 1) % 4, far_y)
    first = jnp.where((far_x + 1) % 4 == third, (far_x + 2) % 4, (far_x + 1) % 4)
    return first, 6 - far_x - third - first, third, far_x


def slot_of(mx, mz):
    x, _, core, y, zl = where_am_i()
    first, second, third, last = columns(x, y)
    d = mz ^ zl
    by_d = jnp.where(d == 1, 8, jnp.where(d == 2, 9, jnp.where(d == 0, 12, 13)))
    by_core = jnp.where(mz % 2 == core, 10, 14) + mz // 2
    in_third = jnp.where(x == y, 8 + mz, by_d)
    in_last = jnp.where(x == y, 12 + mz, by_core)
    rest = jnp.where(mx == third, in_third, in_last)
    return jnp.where(mx == first, mz, jnp.where(mx == second, 4 + mz, rest))


def source_of(slot):
    x, _, core, y, zl = where_am_i()
    first, second, third, last = columns(x, y)
    if slot < 8:
        return (first, second)[slot // 4] * 4 + slot % 4
    if slot < 10:
        return third * 4 + jnp.where(x == y, slot - 8, zl ^ (slot - 7))
    if slot < 12:
        apart = last * 4 + 2 * (slot - 10) + core
        return jnp.where(x == y, third * 4 + slot - 8, apart)
    if slot < 14:
        apart = third * 4 + (zl ^ (0, 3)[slot - 12])
        return jnp.where(x == y, last * 4 + slot - 12, apart)
    return last * 4 + jnp.where(x == y, slot - 12, 2 * (slot - 14) + 1 - core)


def products(labels, amp_in, lad_in, amp_parts, lad_parts, amp, lad, sems, low, groups, unroll, one_block):
    pi = lax.axis_index("pi")
    x, zh, core, y, zl = where_am_i()
    copies = []

    def bring(source, target, h, slot, group):
        wanted = (slot >= low) & (slot < low + 4 * groups)
        at = jnp.where(wanted, slot - low, 0)
        copy = pltpu.make_async_copy(source, target.at[at, h], sems.at[len(copies)])
        copies.append((copy, wanted, group))

    for name, first, (s, d), h, count in amp_parts:
        slot = slot_of((y + 4 - s) % 4, zl ^ d)
        bring(amp_in[name].at[pl.ds(first, count)], amp, pl.ds(h, count), slot, 0)
    for half in range(2):
        for name, first, (s, d, c), h, count in lad_parts:
            if count == 4 and h != half * 4:
                continue
            slot = slot_of((x + 4 - s) % 4, (zh ^ d) * 2 + (core ^ c))
            source = lad_in[name].at[pl.ds(first + half * 4 - h, 4)]
            bring(source, lad, pl.ds(half * 4, 4), slot, half)
    for copy, wanted, _ in copies:
        pl.when(wanted)(copy.start)
    sources = [source_of(low + n) for n in range(4 * groups)]

    label_i = [labels[pi * 2 + i] for i in range(2)]

    def block(hb, carry):
        first = jnp.zeros((128, 256), jnp.float32)
        second = jnp.zeros((128, 256), jnp.float32)
        for g in range(groups):
            weights, left, right = [], [], []
            for k in range(12):
                m, kk = g * 4 + k // 3, k % 3
                part = lad[m, hb, kk]
                low = part[64:96]
                turned = pltpu.roll(low.astype(jnp.float32), 64, 1).astype(jnp.bfloat16)
                weights.append(jnp.concatenate([part[0:64], jnp.concatenate([low, turned], axis=0)], axis=1))
                right.append(amp[m, hb, kk])
            for q in range(6):
                tops = []
                for i in range(2):
                    pair = []
                    for k in (2 * q, 2 * q + 1):
                        m, kk = g * 4 + k // 3, k % 3
                        label = labels[sources[m] * 3 + kk]
                        pair.append(amp[m, hb ^ label_i[i] ^ label, kk][:, i * 64 : i * 64 + 64])
                    tops.append(jnp.concatenate(pair, axis=1))
                left.append(jnp.concatenate(tops, axis=0))
            weight = jnp.concatenate(weights, axis=0)
            first += jnp.dot(jnp.concatenate(left, axis=1), weight, preferred_element_type=jnp.float32)
            second += lax.dot_general(
                jnp.concatenate(right, axis=0), weight, (((0,), (0,)), ((), ())),
                preferred_element_type=jnp.float32,
            )
        one_block(hb, first, second)
        return carry

    for half in range(2):
        for copy, wanted, group in copies:
            if group == half:
                pl.when(wanted)(copy.wait)
        lax.fori_loop(half * 4, half * 4 + 4, block, 0, unroll=unroll)


def early_products(labels, *refs):
    amp_in = dict(zip(AMP_EARLY, refs))
    lad_in = dict(zip(LAD_EARLY, refs[len(AMP_EARLY) :]))
    first_out, second_out, amp, lad, sems = refs[len(AMP_EARLY) + len(LAD_EARLY) :]

    def keep(hb, first, second):
        first_out[hb] = first
        second_out[hb] = second

    amp_parts = [part for part in AMP_PARTS if part[0] in AMP_EARLY]
    lad_parts = [part for part in LAD_PARTS if part[0] in LAD_EARLY]
    products(labels, amp_in, lad_in, amp_parts, lad_parts, amp, lad, sems, 0, 3, 4, keep)


def late_products(labels, first_in, second_in, *refs):
    amp_in = dict(zip(AMP_NAMES, refs))
    lad_in = dict(zip(LAD_NAMES, refs[len(AMP_NAMES) :]))
    out_ref, amp, lad, diff, cross, sems = refs[len(AMP_NAMES) + len(LAD_NAMES) :]
    pi, pj = lax.axis_index("pi"), lax.axis_index("pj")

    def keep(hb, first, second):
        second = second + second_in[hb]
        diff[hb] = 2.0 * (first + first_in[hb]) - second
        cross[hb] = jnp.transpose(second)

    products(labels, amp_in, lad_in, AMP_PARTS, LAD_PARTS, amp, lad, sems, 12, 1, 2, keep)
    label_i = [labels[pi * 2 + i] for i in range(2)]
    label_j = [labels[pj * 3 + j] for j in range(3)]
    tall = []
    for h in range(8):
        row = []
        for i in range(2):
            for j in range(3):
                direct = diff[h ^ label_i[i], i * 64 : i * 64 + 64, j * 64 : j * 64 + 64]
                crossed = cross[h ^ label_j[j], j * 64 : j * 64 + 64, i * 64 : i * 64 + 64]
                row.append(direct - crossed)
        tall.append(jnp.concatenate(row, axis=1).astype(jnp.bfloat16))
    tall = jnp.concatenate(tall, axis=0)
    sides = [jnp.dot(gather_back(p), tall, preferred_element_type=jnp.float32) for p in range(2)]
    for i in range(2):
        for j in range(3):
            at = (i * 3 + j) * 64
            both = jnp.concatenate([s[:, at : at + 64] for s in sides], axis=1)
            for v in range(32):
                out_ref[i, j, :, v * 128 : v * 128 + 128] = both[v * 8 : v * 8 + 8].astype(jnp.bfloat16)


AMP_PARTS = [
    ("a", 0, (0, 0), 0, 8), ("z1", 0, (0, 1), 0, 8), ("z2", 0, (0, 2), 0, 8), ("z3", 0, (0, 3), 0, 8),
    ("yo+", 0, (1, 0), 0, 8), ("yo-", 0, (3, 0), 0, 8), ("fo", 0, (2, 0), 0, 8),
    ("yq+", 0, (1, 1), 0, 8), ("yq+", 8, (1, 2), 0, 8), ("yq-", 0, (3, 1), 0, 8), ("yq-", 8, (3, 2), 0, 8),
    ("f1", 0, (2, 1), 0, 8), ("f2", 0, (2, 2), 0, 8),
    ("y3+", 0, (1, 3), 0, 8), ("y3-", 0, (3, 3), 0, 8), ("f3", 0, (2, 3), 0, 8),
]
LAD_PARTS = [
    ("l", 0, (0, 0, 0), 0, 8), ("xo+", 0, (1, 0, 0), 0, 8), ("xo-", 0, (3, 0, 0), 0, 8), ("fxo", 0, (2, 0, 0), 0, 8),
    ("zh", 0, (0, 1, 0), 0, 8), ("xz+", 0, (1, 1, 0), 0, 8), ("xz-", 0, (3, 1, 0), 0, 8),
    ("fxz+", 0, (2, 1, 0), 0, 4), ("fxz-", 0, (2, 1, 0), 4, 4),
    ("c1", 0, (0, 0, 1), 0, 8), ("c1", 8, (1, 0, 1), 0, 8), ("c1", 16, (3, 0, 1), 0, 8),
    ("c1", 24, (0, 1, 1), 0, 8), ("c1", 32, (1, 1, 1), 0, 8), ("c1", 40, (3, 1, 1), 0, 8),
    ("c2", 0, (2, 0, 1), 0, 8), ("c2", 8, (2, 1, 1), 0, 8),
]
AMP_NAMES = list(dict.fromkeys(part[0] for part in AMP_PARTS))
LAD_NAMES = list(dict.fromkeys(part[0] for part in LAD_PARTS))
AMP_EARLY = [name for name in AMP_NAMES if name not in ("fo", "f3")]
LAD_EARLY = [name for name in LAD_NAMES if name != "c2"]
COPIES = len(AMP_PARTS) + 2 * len(LAD_PARTS)
X_UP, X_DOWN = ("pi", shift_x(1)), ("pi", shift_x(-1))
Y_UP, Y_DOWN, Y_FAR = ("pj", shift_y(1)), ("pj", shift_y(-1)), ("pj", shift_y(2))
Z_ONE, Z_TWO = ("pj", swap_zl(1)), ("pj", swap_zl(2))
Z_HALF, OTHER_CORE = ("pi", SWAP_ZH), ("pi", SWAP_CORE)
SOONER = {"zh": ("z1", "z2")}
PLAN = [
    ("z1", "a", Z_ONE, 0, 1),
    ("z2", "a", Z_TWO, 0, 1),
    ("yo+", "a", Y_UP, 0, 1),
    ("yo-", "a", Y_DOWN, 0, 1),
    ("xo+", "l", X_UP, 0, 1),
    ("zh", "l", Z_HALF, 1, 2),
    ("yq+", ("z1", "z2"), Y_UP, 1, 2),
    ("yq-", ("z1", "z2"), Y_DOWN, 1, 2),
    ("xo-", "l", X_DOWN, 1, 2),
    ("fxo", "xo+", X_UP, 1, 2),
    ("z3", "z2", Z_ONE, 2, 3),
    ("f1", ("yq+", 0, 8), Y_UP, 2, 3),
    ("f2", ("yq-", 8, 16), Y_DOWN, 2, 3),
    ("xz+", "zh", X_UP, 2, 3),
    ("xz-", "zh", X_DOWN, 2, 3),
    ("y3+", "z3", Y_UP, 3, 4),
    ("y3-", "z3", Y_DOWN, 3, 4),
    ("fxz+", ("xz+", 0, 4), X_UP, 3, 4),
    ("fxz-", ("xz-", 4, 8), X_DOWN, 3, 4),
    ("c1", ("l", "xo+", "xo-", "zh", "xz+", "xz-"), OTHER_CORE, 3, 4),
    ("f3", "y3+", Y_UP, 4, 5),
    ("fo", "yo-", Y_DOWN, 4, 5),
    ("c2", ("fxo", "fxz+", "fxz-"), OTHER_CORE, 4, 5),
]
JOINS = {}


def call(kernel, outs, labels, args, spaces, scratch, flops, nbytes, vmem):
    return pl.pallas_call(
        kernel,
        out_shape=outs,
        in_specs=[pl.BlockSpec(memory_space=pltpu.SMEM)] + [pl.BlockSpec(memory_space=s) for s in spaces],
        out_specs=[pl.BlockSpec(memory_space=pltpu.VMEM)] * len(outs),
        scratch_shapes=scratch,
        compiler_params=pltpu.CompilerParams(vmem_limit_bytes=vmem * 1024 * 1024),
        cost_estimate=pl.CostEstimate(flops=flops, bytes_accessed=nbytes, transcendentals=0),
    )(labels, *args)


def lay_out(labels, *args):
    scratch = [pltpu.VMEM(arg.shape, arg.dtype) for arg in args] + [pltpu.SemaphoreType.DMA((3,))]
    outs = [jax.ShapeDtypeStruct((8, 3, rows, 128), jnp.bfloat16) for rows in (64, 96)]
    return call(prepare, outs, labels, args, [pl.ANY] * 3, scratch, 2 * 10**9, 3 * 10**6, 60)


def slots(count):
    return [pltpu.VMEM((count, 8, 3, rows, 128), jnp.bfloat16) for rows in (64, 96)]


def begin(labels, got):
    args = [fetch(got, name) for name in AMP_EARLY + LAD_EARLY]
    outs = [jax.ShapeDtypeStruct((8, 128, 256), jnp.float32)] * 2
    scratch = slots(12) + [pltpu.SemaphoreType.DMA((COPIES,))]
    return call(early_products, outs, labels, args, [pl.ANY] * len(args), scratch, 7 * 10**9, 12 * 10**6, 22)


def finish(labels, got, sums):
    args = [fetch(got, name) for name in AMP_NAMES + LAD_NAMES]
    outs = [jax.ShapeDtypeStruct((2, 3, 8, NVI * NVI), jnp.bfloat16)]
    scratch = slots(4) + [
        pltpu.VMEM((8, 128, 256), jnp.float32),
        pltpu.VMEM((8, 256, 128), jnp.float32),
        pltpu.SemaphoreType.DMA((COPIES,)),
    ]
    spaces = [pltpu.VMEM] * 2 + [pl.ANY] * len(args)
    return call(late_products, outs, labels, [*sums, *args], spaces, scratch, 2 * 10**9, 4 * 10**6, 20)[0]


def fetch(got, source):
    if isinstance(source, str) and source in JOINS:
        source = JOINS[source]
    if isinstance(source, str):
        return got[source]
    if isinstance(source[1], int):
        return got[source[0]][source[1] : source[2]]
    return jnp.concatenate([fetch(got, part) for part in source], axis=0)


def on_device(amplitudes, coulomb, exchange, occ_irrep):
    got = dict(zip("al", lay_out(occ_irrep, amplitudes, coulomb, exchange)))
    ends = {name: end for name, _, _, _, end in PLAN}
    starts = {name: start for name, _, _, start, _ in PLAN}
    for name, source, (axis, pairs), start, _ in sorted(PLAN, key=lambda step: step[3]):
        before = [n for n in ends if ends[n] <= start]
        last = SOONER.get(name) or [n for n in before if not any(ends[n] <= starts[m] for m in before)]
        value = fetch(got, source)
        if last:
            value = lax.optimization_barrier((value, *[got[n] for n in last]))[0]
        got[name] = lax.ppermute(value, axis, pairs)
    return finish(occ_irrep, got, begin(occ_irrep, got))


def solution(mesh):
    placed = (P("pi", "pj", None, None), P("pi", "pj", None, None), P("pi", "pj", None, None), P())
    return jax.shard_map(
        on_device, mesh=mesh, in_specs=placed, out_specs=P("pi", "pj", None, None), check_vma=False
    )
```
